512 devices in a mesh: dp: 4 (over x), ctx: 16 (over z_lo, y), section: 8 (over z_hi, core).
Axes of the slice: x: 4, y: 4, z: 16 (z_hi: 4, z_lo: 4; z = z_hi * 4 + z_lo), core: 2. Of those that a mesh axis runs over, the one named last changes fastest.
Arguments:
- queries: bfloat16 [4, 8, 2048, 4096], P('dp', 'section', 'ctx'), may hold values from -20 to 20
- keys: bfloat16 [4, 8, 2048, 512], P('dp', 'section', 'ctx'), may hold values from -20 to 20
- values: bfloat16 [4, 8, 2048, 512], P('dp', 'section', 'ctx'), may hold values from -6 to 6
- out_grad: bfloat16 [4, 8, 2048, 4096], P('dp', 'section', 'ctx'), may hold values from -6 to 6
- send_slot: int32 [4, 4], replicated, may hold values from 0 to 3, each once within a row
- recv_slot: int32 [4, 4], replicated, may hold values from 0 to 3, each once within a row
- stretch_block: int32 [4, 8, 64], P('dp', 'section'), may hold values from 0 to 63, each once within a row
- doc_ids: int32 [4, 8, 2048], P('dp', 'section'), may hold values from 0 to 31, never falling along the last dimension, each value on 1 to 96 neighbouring positions
Outputs:
- handoff: bfloat16 [4, 8, 2048, 4096], P('dp', 'section', 'ctx')
- query_grad: bfloat16 [4, 8, 2048, 4096], P('dp', 'section', 'ctx')
- key_gradient: bfloat16 [4, 8, 2048, 512], P('dp', 'section', 'ctx')
- value_gradient: bfloat16 [4, 8, 2048, 512], P('dp', 'section', 'ctx')
The draws below stay inside these ranges and needn't reach their ends.
Inputs may be any that keep to these rules, and one draw needn't show every extreme that they name: `send_slot`: each row is a permutation of the replicas' block indices. `recv_slot`: each row is a permutation of the replicas' block indices. `stretch_block`: each sequence's row is a permutation of its 64 position blocks. `doc_ids`: documents are contiguous runs of positions, numbered in order, none longer than 96.
All inputs are finite; a program needn't handle non-finite values.
Results may differ from the reference program's by a relative error of at most 0.025.
Values may be sent and summed in bfloat16 or wider, within the bound.
No kernel may reach another device: no remote copies, remote signals or barrier semaphores. Data moves between devices by JAX's collectives and lax.ppermute only.
A program may use at most 64 MiB of HBM per device.

```python
import math
import jax
import jax.numpy as jnp
import numpy as np
from jax import lax

QUERY_HEADS = 32
KEY_VALUE_HEADS = 4
HEAD_SIZE = 128
TOK_DEV = 128
BLOCK_POSITIONS = 32
REACH_BLOCKS = 4
DBLK = 32
SEQUENCE_LENGTH = 2048
NB = 64
LMAX = 96
N_DP = 4
N_CTX = 16
N_SECTION = 8


def draw_keys(key, part):
    local_key = jax.random.fold_in(key, 3)
    final_result = jnp.clip(jax.random.normal(local_key, (N_DP, N_SECTION, SEQUENCE_LENGTH, KEY_VALUE_HEADS, HEAD_SIZE), jnp.float32), -5.0, 5.0)
    return final_result.reshape(N_DP, N_SECTION, SEQUENCE_LENGTH, KEY_VALUE_HEADS * HEAD_SIZE).astype(jnp.bfloat16)


def draw_queries(key, part):
    local_key = jax.random.fold_in(key, 5)
    head_group = QUERY_HEADS // KEY_VALUE_HEADS
    final_result = jnp.clip(jax.random.normal(local_key, (N_DP, N_SECTION, SEQUENCE_LENGTH, KEY_VALUE_HEADS, head_group, HEAD_SIZE), jnp.float32), -5.0, 5.0)
    return final_result.reshape(N_DP, N_SECTION, SEQUENCE_LENGTH, QUERY_HEADS * HEAD_SIZE).astype(jnp.bfloat16)


def block_levels(rng, extent, pieces, smallest, high):
    gain, own = 1.0, jax.random.fold_in(rng, 6)
    for axis_at, blocks in pieces:
        steps = jnp.exp(jax.random.uniform(jax.random.fold_in(own, axis_at), (blocks,), jnp.float32, smallest / len(pieces), high / len(pieces)))
        gain = gain * jnp.repeat(steps, extent[axis_at] // blocks).reshape([-1 if axis == axis_at else 1 for axis in range(len(extent))])
    return gain


def profile(count, total, most, lean):
    loads = [(1 << 20) // math.isqrt(grade ** lean) + 1 for grade in range(2, count + 1)]
    rest, counts = total - most - (count - 1), [1] * (count - 1)
    while rest > 0:
        candidates = [i for i in range(count - 1) if counts[i] < most]
        pool, budget = sum([loads[i] for i in candidates]), rest
        for i in candidates:
            addition = min(most - counts[i], max(1, budget * loads[i] // pool), rest)
            counts[i] = counts[i] + addition
            rest = rest - addition
    return np.array([most] + counts)


def ragged_sizes(rng, amount, total, most, lean):
    if amount == 2:
        one = jax.random.randint(rng, (), max(1, total - most), min(most, total - 1) + 1)
        return jnp.stack([one, total - one])
    lengths = jnp.asarray(profile(amount, total, most, lean), jnp.int32)
    pairs = (amount - 1) // 2
    giver, receiver = lengths[1:1 + 2 * pairs:2], lengths[2:2 + 2 * pairs:2]
    room = jnp.minimum(giver - 1, most - receiver)
    moved = jax.random.randint(jax.random.fold_in(rng, 1), (pairs,), 0, 1 << 20) % (room + 1)
    lengths = lengths.at[1:1 + 2 * pairs:2].set(giver - moved).at[2:2 + 2 * pairs:2].set(receiver + moved)
    return lengths[jax.random.permutation(jax.random.fold_in(rng, 2), amount)]


def scatter_about(rng, dims, width, limit, pieces=(), kind=jnp.bfloat16):
    factor_of = block_levels(rng, dims, pieces, -0.22, 0.18) if pieces else 1.0
    array = jax.random.normal(rng, dims, jnp.float32) * width * factor_of
    return jnp.minimum(jnp.maximum(array, -limit), limit).astype(kind)


def setup_inputs(seed: int = 0) -> dict:
    streams_of = jax.random.split(jax.random.key(seed), 9)
    return {
        "queries": draw_queries(jax.random.fold_in(streams_of[8], 71), 0),
        "keys": draw_keys(jax.random.fold_in(streams_of[8], 71), 0),
        "values": scatter_about(streams_of[2], (N_DP, N_SECTION, SEQUENCE_LENGTH, KEY_VALUE_HEADS * HEAD_SIZE), 1.0, 6.0, ((0, 4), (1, 8), (2, 16))),
        "out_grad": scatter_about(streams_of[3], (N_DP, N_SECTION, SEQUENCE_LENGTH, QUERY_HEADS * HEAD_SIZE), 1.0, 6.0, ((0, 4), (1, 8), (2, 16))),
        "send_slot": jax.vmap(lambda own: jax.random.permutation(own, N_DP))(jax.random.split(streams_of[4], N_DP)).reshape((N_DP, N_DP)).astype(jnp.int32),
        "recv_slot": jax.vmap(lambda own: jax.random.permutation(own, N_DP))(jax.random.split(streams_of[5], N_DP)).reshape((N_DP, N_DP)).astype(jnp.int32),
        "stretch_block": jax.vmap(lambda own: jax.random.permutation(own, NB))(jax.random.split(streams_of[6], N_DP * N_SECTION)).reshape((N_DP, N_SECTION, NB)).astype(jnp.int32),
        "doc_ids": jax.vmap(lambda own: jnp.searchsorted(jnp.cumsum(ragged_sizes(own, SEQUENCE_LENGTH // (2 * BLOCK_POSITIONS), SEQUENCE_LENGTH, LMAX, 2)), jnp.arange(SEQUENCE_LENGTH), side="right"))(jax.random.split(streams_of[7], N_DP * N_SECTION)).reshape((N_DP, N_SECTION, SEQUENCE_LENGTH)).astype(jnp.int32),
    }


def one_sequence(inputs):
    q_seq, k_seq, v_seq, g_seq, stretch_row, doc_row = inputs
    head_group = QUERY_HEADS // KEY_VALUE_HEADS
    scale = HEAD_SIZE ** -0.5
    slots = jnp.arange(NB, dtype=jnp.int32)
    slot_of = jnp.zeros((NB,), jnp.int32).at[stretch_row].set(slots)

    def by_position(tensor):
        return tensor.reshape(NB, BLOCK_POSITIONS, tensor.shape[-1])[slot_of].reshape(SEQUENCE_LENGTH, tensor.shape[-1])

    query_position = by_position(q_seq)
    key_position = by_position(k_seq)
    value_position = by_position(v_seq)
    gradient_position = by_position(g_seq)
    firsts = jnp.clip(slots - (REACH_BLOCKS - 1), 0, NB - REACH_BLOCKS).astype(jnp.int32)
    covered_range = REACH_BLOCKS * BLOCK_POSITIONS

    def one_block(query_block):
        leading_block = firsts[query_block]
        query_local = lax.dynamic_slice_in_dim(query_position, query_block * BLOCK_POSITIONS, BLOCK_POSITIONS).astype(jnp.float32).reshape(BLOCK_POSITIONS, KEY_VALUE_HEADS, head_group, HEAD_SIZE)
        gradient_local = lax.dynamic_slice_in_dim(gradient_position, query_block * BLOCK_POSITIONS, BLOCK_POSITIONS).astype(jnp.float32).reshape(BLOCK_POSITIONS, KEY_VALUE_HEADS, head_group, HEAD_SIZE)
        key_local = lax.dynamic_slice_in_dim(key_position, leading_block * BLOCK_POSITIONS, covered_range).astype(jnp.float32).reshape(covered_range, KEY_VALUE_HEADS, HEAD_SIZE)
        value_local = lax.dynamic_slice_in_dim(value_position, leading_block * BLOCK_POSITIONS, covered_range).astype(jnp.float32).reshape(covered_range, KEY_VALUE_HEADS, HEAD_SIZE)
        query_at = query_block * BLOCK_POSITIONS + jnp.arange(BLOCK_POSITIONS, dtype=jnp.int32)
        key_at = leading_block * BLOCK_POSITIONS + jnp.arange(covered_range, dtype=jnp.int32)
        allowed = (doc_row[key_at][None, :] == doc_row[query_at][:, None]) & (key_at[None, :] <= query_at[:, None])
        logits = jnp.einsum('qhgd,khd->hgqk', query_local, key_local) * scale
        logits = jnp.where(allowed, logits, -1e30)
        peak = jnp.max(logits, axis=-1, keepdims=True)
        weights = jnp.where(allowed, jnp.exp(logits - peak), 0.0)
        probs = weights / jnp.sum(weights, axis=-1, keepdims=True)
        probs_low = probs.astype(jnp.bfloat16).astype(jnp.float32)
        attn = jnp.einsum('hgqk,khd->qhgd', probs_low, value_local).astype(jnp.bfloat16)
        delta = jnp.einsum('qhgd,qhgd->hgq', gradient_local, attn.astype(jnp.float32))
        dprob = jnp.einsum('qhgd,khd->hgqk', gradient_local, value_local)
        dlogit = (probs * (dprob - delta[..., None])).astype(jnp.bfloat16).astype(jnp.float32)
        q_grad = (jnp.einsum('hgqk,khd->qhgd', dlogit, key_local) * scale).astype(jnp.bfloat16)
        key_summands = jnp.einsum('hgqk,qhgd->khd', dlogit, query_local) * scale
        value_summands = jnp.einsum('hgqk,qhgd->khd', probs_low, gradient_local)
        return (attn.reshape(BLOCK_POSITIONS, QUERY_HEADS * HEAD_SIZE), q_grad.reshape(BLOCK_POSITIONS, QUERY_HEADS * HEAD_SIZE),
                key_summands.reshape(covered_range, KEY_VALUE_HEADS * HEAD_SIZE), value_summands.reshape(covered_range, KEY_VALUE_HEADS * HEAD_SIZE))

    attn_all, qgrad_all, kterm_all, vterm_all = lax.map(one_block, slots)
    device_share = TOK_DEV // BLOCK_POSITIONS
    empty_rows = jnp.zeros((SEQUENCE_LENGTH, KEY_VALUE_HEADS * HEAD_SIZE), jnp.float32)

    def device_part(totals, device):
        def add_block(index, parts):
            query_block = stretch_row[device * device_share + index]
            offset = firsts[query_block] * BLOCK_POSITIONS
            k_part = lax.dynamic_update_slice_in_dim(parts[0], lax.dynamic_slice_in_dim(parts[0], offset, covered_range) + kterm_all[query_block], offset, 0)
            v_part = lax.dynamic_update_slice_in_dim(parts[1], lax.dynamic_slice_in_dim(parts[1], offset, covered_range) + vterm_all[query_block], offset, 0)
            return (k_part, v_part)

        k_part, v_part = lax.fori_loop(0, device_share, add_block, (empty_rows, empty_rows))
        k_low = lax.optimization_barrier(k_part.astype(jnp.bfloat16))
        v_low = lax.optimization_barrier(v_part.astype(jnp.bfloat16))
        return (totals[0] + k_low.astype(jnp.float32), totals[1] + v_low.astype(jnp.float32)), None

    sums, unused = lax.scan(device_part, (empty_rows, empty_rows), jnp.arange(N_CTX, dtype=jnp.int32))

    def by_slot(tensor):
        return tensor.reshape(NB, BLOCK_POSITIONS, tensor.shape[-1])[stretch_row].reshape(SEQUENCE_LENGTH, tensor.shape[-1])

    return (by_slot(attn_all.reshape(SEQUENCE_LENGTH, QUERY_HEADS * HEAD_SIZE)), by_slot(qgrad_all.reshape(SEQUENCE_LENGTH, QUERY_HEADS * HEAD_SIZE)),
            by_slot(sums[0]).astype(jnp.bfloat16), by_slot(sums[1]).astype(jnp.bfloat16))


def reference(queries, keys, values, out_grad, send_slot, recv_slot, stretch_block, doc_ids):
    replica_ids = jnp.arange(N_DP, dtype=jnp.int32)
    source_for = jnp.sum(jnp.where(recv_slot[:, None, :] == replica_ids[None, :, None], replica_ids[None, None, :], 0), axis=2).astype(jnp.int32)
    block_for = send_slot[source_for, replica_ids[:, None]]

    def redeal(tensor):
        row_width = tensor.shape[-1]
        blocks = tensor.reshape(N_DP, N_SECTION, N_CTX, N_DP, DBLK, row_width)
        blocks = jnp.moveaxis(blocks, 3, 1)
        picked = blocks[source_for, block_for]
        picked = jnp.transpose(picked, (0, 2, 3, 1, 4, 5))
        return picked.reshape(N_DP * N_SECTION, SEQUENCE_LENGTH, row_width)

    output_list = lax.map(one_sequence, (redeal(queries), redeal(keys), redeal(values), redeal(out_grad),
                                     stretch_block.reshape(N_DP * N_SECTION, NB), doc_ids.reshape(N_DP * N_SECTION, SEQUENCE_LENGTH)))
    attn = output_list[0].reshape(N_DP, N_SECTION, SEQUENCE_LENGTH, QUERY_HEADS * HEAD_SIZE)
    query_grad = output_list[1].reshape(N_DP, N_SECTION, SEQUENCE_LENGTH, QUERY_HEADS * HEAD_SIZE)
    key_gradient = output_list[2].reshape(N_DP, N_SECTION, SEQUENCE_LENGTH, KEY_VALUE_HEADS * HEAD_SIZE)
    value_gradient = output_list[3].reshape(N_DP, N_SECTION, SEQUENCE_LENGTH, KEY_VALUE_HEADS * HEAD_SIZE)
    handoff = jnp.roll(attn, 1, axis=1)
    return (handoff, query_grad, key_gradient, value_gradient)
```

```python
import jax
import jax.numpy as jnp
from jax import lax
from jax.experimental import pallas as pl
from jax.experimental.pallas import tpu as pltpu
from jax.sharding import PartitionSpec as P

QUERY_HEADS = 32
KEY_VALUE_HEADS = 4
HEAD_SIZE = 128
BLOCK_POSITIONS = 32
N_DP = 4
N_CTX = 16
NB = 64
GROUP = QUERY_HEADS // KEY_VALUE_HEADS
QW = QUERY_HEADS * HEAD_SIZE
KW = KEY_VALUE_HEADS * HEAD_SIZE
G_AT = QW
K_AT = 2 * QW
V_AT = 2 * QW + KW
PAYLOAD = 2 * QW + 2 * KW
HALF = BLOCK_POSITIONS // 2
BEHIND = 3
ENTRIES = N_DP * BEHIND
SCALE = HEAD_SIZE ** (-0.5)

VMEM = pl.BlockSpec(memory_space=pltpu.VMEM)
SMEM = pl.BlockSpec(memory_space=pltpu.SMEM)


def call(kernel, out_shape, in_specs, scratch=(), flops=0, nbytes=1 << 20):
    multi = isinstance(out_shape, (list, tuple))
    return pl.pallas_call(
        kernel,
        out_shape=out_shape,
        in_specs=in_specs,
        out_specs=[VMEM] * len(out_shape) if multi else VMEM,
        scratch_shapes=scratch,
        compiler_params=pltpu.CompilerParams(vmem_limit_bytes=40 * 1024 * 1024),
        cost_estimate=pl.CostEstimate(flops=flops, bytes_accessed=nbytes, transcendentals=0),
    )


def bf16(*shape):
    return jax.ShapeDtypeStruct(shape, jnp.bfloat16)


def replica(me, shift):
    return lax.rem(me + shift + N_DP, N_DP)


def rows(block, half=0, count=BLOCK_POSITIONS):
    return pl.ds(pl.multiple_of(block * BLOCK_POSITIONS + half * HALF, HALF), count)


def pack_kv(me, send, k_ref, v_ref, out_ref):
    r = me[0]
    for u in range(N_DP):
        block = send[r, u]
        for piece in range(N_CTX):
            head, half = piece // 2, piece % 2
            source = k_ref if head < KEY_VALUE_HEADS else v_ref
            column = (head % KEY_VALUE_HEADS) * HEAD_SIZE
            out_ref[u * N_CTX + piece] = source[
                rows(block, half, HALF), column : column + HEAD_SIZE
            ]


def pack_rows(me, send, q_ref, g_ref, k_ref, v_ref, *outs):
    r = me[0]
    for shift in range(N_DP):
        block = send[r, replica(r, shift)]
        outs[shift][:, :G_AT] = q_ref[rows(block), :]
        outs[shift][:, G_AT:K_AT] = g_ref[rows(block), :]
        outs[shift][:, K_AT:V_AT] = k_ref[rows(block), :]
        outs[shift][:, V_AT:] = v_ref[rows(block), :]


def gather_windows(me, recv, stretch, held, out_ref, where_of):
    r = me[0]
    for u in range(N_DP):
        slot = recv[r, u]
        for c in range(N_CTX):
            where_of[stretch[c * N_DP + slot]] = u * N_CTX + c
    for shift in range(N_DP):
        slot = recv[r, replica(r, -shift)]
        for d in range(N_CTX):
            position = stretch[d * N_DP + slot]
            for m in range(BEHIND):
                source = where_of[jnp.maximum(position - BEHIND + m, 0)]
                out_ref[d, shift * BEHIND + m] = held[source]


def sum_windows(me, recv, stretch, held, out_ref, where_of):
    r = me[0]
    for shift in range(N_DP):
        slot = recv[r, replica(r, -shift)]
        for d in range(N_CTX):
            where_of[stretch[d * N_DP + slot]] = d * ENTRIES + shift * BEHIND
    for s in range(NB):
        position = stretch[s]
        total = jnp.zeros((HALF, HEAD_SIZE), jnp.float32)
        for ahead in range(1, BEHIND + 1):
            reader = position + ahead
            entry = where_of[jnp.minimum(reader, NB - 1)] + (BEHIND - ahead)
            term = held[entry].astype(jnp.float32)
            total = total + jnp.where(reader < NB, term, 0.0)
        out_ref[s] = total.astype(jnp.bfloat16)


def finish(held, own, k_out, v_out):
    for piece in range(N_CTX):
        head, half = piece // 2, piece % 2
        target = k_out if head < KEY_VALUE_HEADS else v_out
        column = (head % KEY_VALUE_HEADS) * HEAD_SIZE
        for j in range(N_DP):
            at = j * BLOCK_POSITIONS + half * HALF
            target[at : at + HALF, column : column + HEAD_SIZE] = (
                held[piece * N_DP + j].astype(jnp.float32)
                + own[at : at + HALF, head * HEAD_SIZE : (head + 1) * HEAD_SIZE]
            ).astype(jnp.bfloat16)


def dot(a, b, dims):
    return lax.dot_general(a, b, ((dims[:1], dims[1:]), ((), ())), preferred_element_type=jnp.float32)


def attend(me, recv, x0, x1, x2, x3, low_ref, win, attn, dq, sends, own):
    r = me[0]
    span = (BEHIND + 1) * BLOCK_POSITIONS
    many = GROUP * BLOCK_POSITIONS
    key_at = lax.broadcasted_iota(jnp.int32, (span, many), 0)
    query_at = lax.broadcasted_iota(jnp.int32, (span, many), 1) % BLOCK_POSITIONS + BEHIND * BLOCK_POSITIONS
    for shift, x in enumerate((x0, x1, x2, x3)):
        slot = recv[r, replica(r, -shift)]
        allowed = (key_at >= low_ref[shift : shift + 1, :]) & (key_at <= query_at)

        def head_step(h, carry, shift=shift, x=x, slot=slot, allowed=allowed):
            def window(first_piece, own_at):
                parts = [
                    win[first_piece + half, shift * BEHIND + m]
                    for m in range(BEHIND)
                    for half in range(2)
                ]
                mine = pl.ds(pl.multiple_of(own_at + h * HEAD_SIZE, HEAD_SIZE), HEAD_SIZE)
                return jnp.concatenate(parts + [x[:, mine]], axis=0)

            def stacked(base):
                parts = [
                    x[:, pl.ds(pl.multiple_of(base + h * (GROUP * HEAD_SIZE) + i * HEAD_SIZE, HEAD_SIZE), HEAD_SIZE)]
                    for i in range(GROUP)
                ]
                return jnp.concatenate(parts, axis=0)

            key = window(2 * h, K_AT)
            value = window(2 * (h + KEY_VALUE_HEADS), V_AT)
            query = stacked(0)
            grad = stacked(G_AT)
            logits = jnp.where(allowed, dot(key, query, (1, 1)) * SCALE, -1e30)
            peak = jnp.max(logits, axis=0, keepdims=True)
            weights = jnp.where(allowed, jnp.exp(logits - peak), 0.0)
            probs = weights * (1.0 / jnp.sum(weights, axis=0, keepdims=True))
            low = probs.astype(jnp.bfloat16)
            out = dot(low, value, (0, 0)).astype(jnp.bfloat16)
            dprob = dot(value, grad, (1, 1))
            delta = jnp.sum(low.astype(jnp.float32) * dprob, axis=0, keepdims=True)
            dlogit = (probs * (dprob - delta)).astype(jnp.bfloat16)
            q_grad = (dot(dlogit, key, (0, 0)) * SCALE).astype(jnp.bfloat16)
            for i in range(GROUP):
                column = pl.ds(pl.multiple_of(h * (GROUP * HEAD_SIZE) + i * HEAD_SIZE, HEAD_SIZE), HEAD_SIZE)
                part = slice(i * BLOCK_POSITIONS, (i + 1) * BLOCK_POSITIONS)
                attn[rows(slot), column] = out[part]
                dq[rows(slot), column] = q_grad[part]
            for which, term in (
                (0, dot(dlogit, query, (1, 0)) * SCALE),
                (KEY_VALUE_HEADS, dot(low, grad, (1, 0))),
            ):
                term_low = term[: BEHIND * BLOCK_POSITIONS].astype(jnp.bfloat16)
                for m in range(BEHIND):
                    for half in range(2):
                        at = m * BLOCK_POSITIONS + half * HALF
                        sends[2 * (h + which) + half, shift * BEHIND + m] = term_low[at : at + HALF]
                column = pl.ds(pl.multiple_of((h + which) * HEAD_SIZE, HEAD_SIZE), HEAD_SIZE)
                own[rows(slot), column] = term[BEHIND * BLOCK_POSITIONS :]
            return carry

        lax.fori_loop(0, KEY_VALUE_HEADS, head_step, 0)


def first_keys(stretch, docs, recv_row, me_dp, me_ctx):
    blocks = jnp.stack(
        [
            lax.dynamic_index_in_dim(
                stretch,
                me_ctx * N_DP + lax.dynamic_index_in_dim(recv_row, replica(me_dp, -shift), 0, False),
                0,
                False,
            )
            for shift in range(N_DP)
        ]
    )
    mine = jnp.take(docs.reshape(NB, BLOCK_POSITIONS), blocks, axis=0)
    start = jnp.sum((docs[None, None, :] < mine[:, :, None]).astype(jnp.int32), axis=-1)
    low = start - (blocks[:, None] - BEHIND) * BLOCK_POSITIONS
    return jnp.tile(low, (1, GROUP))


def on_device(queries, keys, values, out_grad, send_slot, recv_slot, stretch_block, doc_ids):
    me_dp = lax.axis_index("dp")
    me_ctx = lax.axis_index("ctx")
    me = me_dp.reshape(1).astype(jnp.int32)
    q, k, v, g = queries[0, 0], keys[0, 0], values[0, 0], out_grad[0, 0]
    stretch = stretch_block[0, 0]
    docs = doc_ids[0, 0]
    tokens = q.shape[0]

    kv_send = call(pack_kv, bf16(N_DP * N_CTX, HALF, HEAD_SIZE), [SMEM, SMEM, VMEM, VMEM])(
        me, send_slot, k, v
    )
    held = lax.all_to_all(kv_send, ("dp", "ctx"), 0, 0, tiled=True)
    payloads = call(
        pack_rows, [bf16(BLOCK_POSITIONS, PAYLOAD)] * N_DP, [SMEM, SMEM] + [VMEM] * 4, nbytes=9 << 19
    )(me, send_slot, q, g, k, v)
    blocks = [payloads[0]] + [
        lax.ppermute(payloads[shift], "dp", [(i, (i + shift) % N_DP) for i in range(N_DP)])
        for shift in range(1, N_DP)
    ]
    low = first_keys(
        stretch, docs, lax.dynamic_index_in_dim(recv_slot, me_dp, 0, False), me_dp, me_ctx
    )
    table = [pltpu.SMEM((NB,), jnp.int32)]
    wanted = call(
        gather_windows, bf16(N_CTX, ENTRIES, HALF, HEAD_SIZE), [SMEM] * 3 + [VMEM], table
    )(me, recv_slot, stretch, held)
    windows = lax.all_to_all(wanted, "ctx", 0, 0, tiled=True)
    attn, q_grad, sends, own = call(
        attend,
        [
            bf16(tokens, QW),
            bf16(tokens, QW),
            bf16(N_CTX, ENTRIES, HALF, HEAD_SIZE),
            jax.ShapeDtypeStruct((tokens, 2 * KW), jnp.float32),
        ],
        [SMEM, SMEM] + [VMEM] * 6,
        flops=1 << 30,
        nbytes=6 << 20,
    )(me, recv_slot, *blocks, low, windows)
    handoff = lax.ppermute(
        attn, "section", [(i, (i + 1) % lax.axis_size("section")) for i in range(lax.axis_size("section"))]
    )
    partial = lax.all_to_all(sends, "ctx", 0, 0, tiled=True)
    summed = call(
        sum_windows, bf16(NB, HALF, HEAD_SIZE), [SMEM] * 3 + [VMEM], table
    )(me, recv_slot, stretch, partial.reshape(N_CTX * ENTRIES, HALF, HEAD_SIZE))
    back = lax.all_to_all(summed.reshape(N_CTX, N_DP, HALF, HEAD_SIZE), "ctx", 0, 0, tiled=True)
    k_grad, v_grad = call(finish, [bf16(tokens, KW)] * 2, [VMEM] * 2)(
        back.reshape(NB, HALF, HEAD_SIZE), own
    )
    return handoff[None, None], q_grad[None, None], k_grad[None, None], v_grad[None, None]


def solution(mesh):
    tokens = P("dp", "section", "ctx", None)
    row = P("dp", "section", None)
    return jax.shard_map(
        on_device,
        mesh=mesh,
        in_specs=(tokens, tokens, tokens, tokens, P(), P(), row, row),
        out_specs=(tokens, tokens, tokens, tokens),
        check_vma=False,
    )
```

```python
import math

import jax
import jax.numpy as jnp
from jax import lax
from jax.experimental import pallas as pl
from jax.experimental.pallas import tpu as pltpu
from jax.sharding import PartitionSpec as P

QUERY_HEADS = 32
KEY_VALUE_HEADS = 4
HEAD_SIZE = 128
BLOCK_POSITIONS = 32
N_DP = 4
N_CTX = 16
NB = 64
GROUP = QUERY_HEADS // KEY_VALUE_HEADS
QW = QUERY_HEADS * HEAD_SIZE
KW = KEY_VALUE_HEADS * HEAD_SIZE
K_AT = QW
V_AT = QW + KW
G_AT = QW + 2 * KW
PAYLOAD = 2 * QW + 2 * KW
PIECES = 2 * KEY_VALUE_HEADS
BEHIND = 3
ENTRIES = N_DP * BEHIND
SCALE = HEAD_SIZE ** (-0.5)
LOG2_E = math.log2(math.e)
SPAN = (BEHIND + 1) * BLOCK_POSITIONS

VMEM = pl.BlockSpec(memory_space=pltpu.VMEM)
SMEM = pl.BlockSpec(memory_space=pltpu.SMEM)
ANY = pl.BlockSpec(memory_space=pl.ANY)
HBM = pl.BlockSpec(memory_space=pltpu.HBM)


def call(
    kernel, out_shape, in_specs, scratch=(), flops=0, nbytes=1 << 20, out_space=VMEM, aliases={}, limit=40
):
    if isinstance(out_shape, list) and not isinstance(out_space, list):
        out_space = [out_space] * len(out_shape)
    return pl.pallas_call(
        kernel,
        out_shape=out_shape,
        in_specs=in_specs,
        out_specs=out_space,
        scratch_shapes=scratch,
        input_output_aliases=aliases,
        compiler_params=pltpu.CompilerParams(vmem_limit_bytes=limit << 20),
        cost_estimate=pl.CostEstimate(flops=flops, bytes_accessed=nbytes, transcendentals=0),
    )


def bf16(*shape):
    return jax.ShapeDtypeStruct(shape, jnp.bfloat16)


def replica(me, shift):
    return lax.rem(me + shift + N_DP, N_DP)


def rows(block):
    return pl.ds(pl.multiple_of(block * BLOCK_POSITIONS, BLOCK_POSITIONS), BLOCK_POSITIONS)


def pack(me, send, q_ref, g_ref, k_ref, v_ref, pieces, own, plus, minus, far, far_g, k_rows, v_rows, sems):
    r = me[0]
    copies = [
        pltpu.make_async_copy(k_ref, k_rows, sems.at[0]),
        pltpu.make_async_copy(v_ref, v_rows, sems.at[1]),
    ]
    for shift, main, grad in ((1, plus, plus), (3, minus, minus), (2, far, far_g), (0, own, own)):
        source = rows(send[r, replica(r, shift)])
        for ref, target, column in ((q_ref, main, 0), (g_ref, grad, 0 if shift == 2 else G_AT)):
            copies.append(
                pltpu.make_async_copy(
                    ref.at[source], target.at[:, column : column + QW], sems.at[len(copies)]
                )
            )
    for copy in copies:
        copy.start()
    copies[0].wait()
    copies[1].wait()
    for u in range(N_DP):
        block = send[r, u]
        for piece in range(PIECES):
            source = k_rows if piece < KEY_VALUE_HEADS else v_rows
            column = (piece % KEY_VALUE_HEADS) * HEAD_SIZE
            part = source[rows(block), column : column + HEAD_SIZE]
            for c in range(piece, N_CTX, PIECES):
                pieces[u * N_CTX + c] = part
    for shift, target in ((1, plus), (3, minus), (2, far), (0, own)):
        block = send[r, replica(r, shift)]
        target[:, K_AT:V_AT] = k_rows[rows(block), :]
        target[:, V_AT:G_AT] = v_rows[rows(block), :]
    for copy in copies[2:]:
        copy.wait()


def gather_windows(me, recv, stretch, held, plus, minus, docs, out_ref, where_of):
    r = me[0]
    first = (me[1] // PIECES) * PIECES
    for u in range(N_DP):
        slot = recv[r, u]
        for c in range(N_CTX):
            where_of[stretch[c * N_DP + slot]] = u * N_CTX + c
    for shift in range(N_DP):
        slot = recv[r, replica(r, -shift)]
        for d in range(PIECES):
            position = stretch[(first + d) * N_DP + slot]
            for m in range(BEHIND):
                source = where_of[jnp.maximum(position - BEHIND + m, 0)]
                out_ref[d, shift * BEHIND + m] = held[source]


def sum_windows(me, recv, stretch, held, handoff, out_ref, where_of):
    r = me[0]
    first = (me[1] // PIECES) * PIECES
    for position in range(NB):
        where_of[position] = -1
    for shift in range(N_DP):
        slot = recv[r, replica(r, -shift)]
        for d in range(PIECES):
            where_of[stretch[(first + d) * N_DP + slot]] = d * ENTRIES + shift * BEHIND
    for s in range(NB):
        position = stretch[s]
        total = jnp.zeros((BLOCK_POSITIONS, HEAD_SIZE), jnp.float32)
        for ahead in range(1, BEHIND + 1):
            reader = position + ahead
            entry = where_of[jnp.minimum(reader, NB - 1)]
            here = (reader < NB) & (entry >= 0)
            term = held[jnp.maximum(entry, 0) + (BEHIND - ahead)].astype(jnp.float32)
            total = total + jnp.where(here, term, 0.0)
        out_ref[s] = total.astype(jnp.bfloat16)


def finish(held, own, k_out, v_out):
    for piece in range(PIECES):
        target = k_out if piece < KEY_VALUE_HEADS else v_out
        column = (piece % KEY_VALUE_HEADS) * HEAD_SIZE
        for j in range(N_DP):
            at = slice(j * BLOCK_POSITIONS, (j + 1) * BLOCK_POSITIONS)
            total = own[at, piece * HEAD_SIZE : (piece + 1) * HEAD_SIZE]
            for c in range(piece, N_CTX, PIECES):
                total = total + held[c * N_DP + j].astype(jnp.float32)
            target[at, column : column + HEAD_SIZE] = total.astype(jnp.bfloat16)


def dot(a, b, dims):
    return lax.dot_general(a, b, ((dims[:1], dims[1:]), ((), ())), preferred_element_type=jnp.float32)


def window_of(win, x, shift, head, own_at):
    parts = [win[head, shift * BEHIND + m] for m in range(BEHIND)]
    return jnp.concatenate(parts + [x[:, own_at : own_at + HEAD_SIZE]], axis=0)


def stacked(x, base, head):
    at = base + head * GROUP * HEAD_SIZE
    parts = [x[:, at + i * HEAD_SIZE : at + (i + 1) * HEAD_SIZE] for i in range(GROUP)]
    return jnp.concatenate(parts, axis=0)


def unstack(target, slot, head, tall):
    for i in range(GROUP):
        at = (head * GROUP + i) * HEAD_SIZE
        target[rows(slot), at : at + HEAD_SIZE] = tall[i * BLOCK_POSITIONS : (i + 1) * BLOCK_POSITIONS]


def forward(me, recv, stretch, own_block, plus, far, minus, docs, win, *outs):
    r = me[0]
    key_at = lax.broadcasted_iota(jnp.int32, (SPAN, SPAN), 0)
    query_at = lax.broadcasted_iota(jnp.int32, (SPAN, SPAN), 1) % BLOCK_POSITIONS
    causal = key_at <= query_at + BEHIND * BLOCK_POSITIONS
    for shift, x in enumerate((own_block, plus, far, minus)):
        slot = recv[r, replica(r, -shift)]
        row = docs[pl.ds(stretch[me[1] * N_DP + slot], 1), :]
        key_doc = jnp.transpose(jnp.broadcast_to(row, (SPAN, SPAN)))
        query_doc = jnp.tile(row[:, BEHIND * BLOCK_POSITIONS :], (1, SPAN // BLOCK_POSITIONS))
        bias = jnp.where((key_doc == query_doc) & causal, 0.0, -1e30)
        bias = jnp.concatenate([bias, bias], axis=1)
        for head in range(KEY_VALUE_HEADS):
            key = window_of(win, x, shift, head, K_AT + head * HEAD_SIZE)
            value = window_of(win, x, shift, head + KEY_VALUE_HEADS, V_AT + head * HEAD_SIZE)
            logits = dot(key, stacked(x, 0, head), (1, 1)) * (SCALE * LOG2_E) + bias
            weights = jnp.exp2(logits - jnp.max(logits, axis=0, keepdims=True))
            probs = weights * (1.0 / jnp.sum(weights, axis=0, keepdims=True))
            outs[-1][shift * KEY_VALUE_HEADS + head] = probs
            out = dot(probs.astype(jnp.bfloat16), value, (0, 0)).astype(jnp.bfloat16)
            unstack(outs[0], slot, head, out)


def backward(me, recv, own_block, plus, far, minus, far_g, win, probs_in, dq, sends, own):
    r = me[0]
    for shift, x in enumerate((own_block, plus, far, minus)):
        slot = recv[r, replica(r, -shift)]
        for head in range(KEY_VALUE_HEADS):
            key = window_of(win, x, shift, head, K_AT + head * HEAD_SIZE)
            value = window_of(win, x, shift, head + KEY_VALUE_HEADS, V_AT + head * HEAD_SIZE)
            query = stacked(x, 0, head)
            grad = stacked(far_g, 0, head) if shift == 2 else stacked(x, G_AT, head)
            probs = probs_in[shift * KEY_VALUE_HEADS + head]
            low = probs.astype(jnp.bfloat16)
            dprob = dot(value, grad, (1, 1))
            delta = jnp.sum(low.astype(jnp.float32) * dprob, axis=0, keepdims=True)
            dlogit = (probs * (dprob - delta)).astype(jnp.bfloat16)
            unstack(dq, slot, head, (dot(dlogit, key, (0, 0)) * SCALE).astype(jnp.bfloat16))
            for column, term in (
                (head, dot(dlogit, query, (1, 0)) * SCALE),
                (head + KEY_VALUE_HEADS, dot(low, grad, (1, 0))),
            ):
                term_low = term[: BEHIND * BLOCK_POSITIONS].astype(jnp.bfloat16)
                for m in range(BEHIND):
                    sends[column, shift * BEHIND + m] = term_low[m * BLOCK_POSITIONS : (m + 1) * BLOCK_POSITIONS]
                own[rows(slot), column * HEAD_SIZE : (column + 1) * HEAD_SIZE] = term[BEHIND * BLOCK_POSITIONS :]


def window_docs(docs):
    padded = jnp.concatenate([jnp.full((BEHIND * BLOCK_POSITIONS,), -1, jnp.int32), docs])
    padded = padded.reshape(NB + BEHIND, BLOCK_POSITIONS)
    return jnp.concatenate([padded[m : m + NB] for m in range(BEHIND + 1)], axis=1)


def on_device(queries, keys, values, out_grad, send_slot, recv_slot, stretch_block, doc_ids):
    me = jnp.stack([lax.axis_index("dp"), lax.axis_index("ctx")]).astype(jnp.int32)
    q, k, v, g = queries[0, 0], keys[0, 0], values[0, 0], out_grad[0, 0]
    stretch = stretch_block[0, 0]
    tokens = q.shape[0]
    n_section = lax.axis_size("section")

    pieces, own_block, plus, minus, far, far_g = call(
        pack,
        [bf16(N_DP * N_CTX, BLOCK_POSITIONS, HEAD_SIZE)]
        + [bf16(BLOCK_POSITIONS, width) for width in (PAYLOAD, PAYLOAD, PAYLOAD, G_AT, QW)],
        [SMEM, SMEM] + [ANY] * 4,
        [pltpu.VMEM((tokens, KW), jnp.bfloat16)] * 2 + [pltpu.SemaphoreType.DMA((2 + 2 * N_DP,))],
        nbytes=9 << 19,
    )(me, send_slot, *(pltpu.with_memory_space_constraint(x, pltpu.HBM) for x in (q, g, k, v)))
    held = lax.all_to_all(pieces, ("dp", "ctx"), 0, 0, tiled=True)
    ahead = [(i, (i + 1) % N_DP) for i in range(N_DP)]
    behind = [(i, (i - 1) % N_DP) for i in range(N_DP)]
    plus = lax.ppermute(plus, "dp", ahead)
    minus = lax.ppermute(minus, "dp", behind)
    far = lax.ppermute(far, "dp", [(i, (i + 2) % N_DP) for i in range(N_DP)])
    far_g = lax.ppermute(far_g, "dp", [(i, (i + 2) % N_DP) for i in range(N_DP)])
    docs = window_docs(doc_ids[0, 0])
    table = [pltpu.SMEM((NB,), jnp.int32)]
    wanted = call(
        gather_windows, bf16(PIECES, ENTRIES, BLOCK_POSITIONS, HEAD_SIZE), [SMEM] * 3 + [VMEM] + [ANY] * 3, table
    )(me, recv_slot, stretch, held, plus, minus, docs)
    halves = [list(range(at, at + PIECES)) for at in range(0, N_CTX, PIECES)]
    windows = lax.all_to_all(wanted, "ctx", 0, 0, tiled=True, axis_index_groups=halves)
    attn, probs = call(
        forward,
        [bf16(tokens, QW), jax.ShapeDtypeStruct((N_DP * KEY_VALUE_HEADS, SPAN, GROUP * BLOCK_POSITIONS), jnp.float32)],
        [SMEM] * 3 + [VMEM] * 6,
        flops=1 << 29,
        nbytes=6 << 20,
    )(me, recv_slot, stretch, own_block, plus, far, minus, docs, windows)
    onward = [(i, (i + 1) % n_section) for i in range(n_section)]
    odd = lax.axis_index("section") % 2 == 1
    hop = lax.ppermute(attn, "section", [(i, (i + 2) % n_section) for i in range(1, n_section, 2)])
    handoff = lax.ppermute(jnp.where(odd, hop, attn), "section", [(i, i ^ 1) for i in range(n_section)])
    q_grad, sends, own = call(
        backward,
        [
            bf16(tokens, QW),
            bf16(PIECES, ENTRIES, BLOCK_POSITIONS, HEAD_SIZE),
            jax.ShapeDtypeStruct((tokens, 2 * KW), jnp.float32),
        ],
        [SMEM] * 2 + [VMEM] * 7,
        flops=1 << 30,
        nbytes=6 << 20,
    )(me, recv_slot, own_block, plus, far, minus, far_g, windows, probs)
    partial = lax.all_to_all(sends, "ctx", 0, 0, tiled=True, axis_index_groups=halves)
    summed = call(
        sum_windows,
        bf16(NB, BLOCK_POSITIONS, HEAD_SIZE),
        [SMEM] * 3 + [VMEM] + [ANY],
        table,
    )(me, recv_slot, stretch, partial.reshape(PIECES * ENTRIES, BLOCK_POSITIONS, HEAD_SIZE), handoff)
    back = lax.all_to_all(summed.reshape(N_CTX, N_DP, BLOCK_POSITIONS, HEAD_SIZE), "ctx", 0, 0, tiled=True)
    k_grad, v_grad = call(finish, [bf16(tokens, KW)] * 2, [VMEM] * 2)(
        back.reshape(NB, BLOCK_POSITIONS, HEAD_SIZE), own
    )
    return handoff[None, None], q_grad[None, None], k_grad[None, None], v_grad[None, None]


def solution(mesh):
    tokens = P("dp", "section", "ctx", None)
    row = P("dp", "section", None)
    return jax.shard_map(
        on_device,
        mesh=mesh,
        in_specs=(tokens, tokens, tokens, tokens, P(), P(), row, row),
        out_specs=(tokens, tokens, tokens, tokens),
        check_vma=False,
    )
```

```python
import math

import jax
import jax.numpy as jnp
from jax import lax
from jax.experimental import pallas as pl
from jax.experimental.pallas import tpu as pltpu
from jax.sharding import PartitionSpec as P

QUERY_HEADS = 32
KEY_VALUE_HEADS = 4
HEAD_SIZE = 128
BLOCK_POSITIONS = 32
N_DP = 4
N_CTX = 16
NB = 64
GROUP = QUERY_HEADS // KEY_VALUE_HEADS
QW = QUERY_HEADS * HEAD_SIZE
KW = KEY_VALUE_HEADS * HEAD_SIZE
K_AT = QW
V_AT = QW + KW
PAYLOAD = QW + 2 * KW
PIECES = 2 * KEY_VALUE_HEADS
SPLIT = 3
BEHIND = 3
ENTRIES = N_DP * BEHIND
SCALE = HEAD_SIZE ** (-0.5)
LOG2_E = math.log2(math.e)
SPAN = (BEHIND + 1) * BLOCK_POSITIONS

VMEM = pl.BlockSpec(memory_space=pltpu.VMEM)
SMEM = pl.BlockSpec(memory_space=pltpu.SMEM)
ANY = pl.BlockSpec(memory_space=pl.ANY)
HBM = pl.BlockSpec(memory_space=pltpu.HBM)


def call(
    kernel, out_shape, in_specs, scratch=(), flops=0, nbytes=1 << 20, out_space=VMEM, aliases={}, limit=40
):
    if isinstance(out_shape, list) and not isinstance(out_space, list):
        out_space = [out_space] * len(out_shape)
    return pl.pallas_call(
        kernel,
        out_shape=out_shape,
        in_specs=in_specs,
        out_specs=out_space,
        scratch_shapes=scratch,
        input_output_aliases=aliases,
        compiler_params=pltpu.CompilerParams(vmem_limit_bytes=limit << 20),
        cost_estimate=pl.CostEstimate(flops=flops, bytes_accessed=nbytes, transcendentals=0),
    )


def bf16(*shape):
    return jax.ShapeDtypeStruct(shape, jnp.bfloat16)


def replica(me, shift):
    return lax.rem(me + shift + N_DP, N_DP)


def rows(block):
    return pl.ds(pl.multiple_of(block * BLOCK_POSITIONS, BLOCK_POSITIONS), BLOCK_POSITIONS)


def pack(me, send, q_ref, g_ref, k_ref, v_ref, pieces, *refs):
    mains, grads, (k_rows, v_rows, sems) = refs[:N_DP], refs[N_DP : 2 * N_DP], refs[2 * N_DP :]
    r = me[0]
    copies = [
        pltpu.make_async_copy(k_ref, k_rows, sems.at[0]),
        pltpu.make_async_copy(v_ref, v_rows, sems.at[1]),
    ]
    for shift in (1, 3, 2, 0):
        source = rows(send[r, replica(r, shift)])
        for ref, target in ((q_ref, mains[shift].at[:, :QW]), (g_ref, grads[shift])):
            copies.append(pltpu.make_async_copy(ref.at[source], target, sems.at[len(copies)]))
    for copy in copies:
        copy.start()
    copies[0].wait()
    copies[1].wait()
    for u in range(N_DP):
        block = send[r, u]
        for piece in range(PIECES):
            source = k_rows if piece < KEY_VALUE_HEADS else v_rows
            column = (piece % KEY_VALUE_HEADS) * HEAD_SIZE
            part = source[rows(block), column : column + HEAD_SIZE]
            for c in range(piece, N_CTX, PIECES):
                pieces[u * N_CTX + c] = part
    for shift, target in enumerate(mains):
        block = send[r, replica(r, shift)]
        target[:, K_AT:V_AT] = k_rows[rows(block), :]
        target[:, V_AT:] = v_rows[rows(block), :]
    for copy in copies[2:]:
        copy.wait()


def gather_windows(me, recv, stretch, held, after, before, out_ref, where_of):
    r = me[0]
    first = (me[1] // PIECES) * PIECES
    for u in range(N_DP):
        slot = recv[r, u]
        for c in range(N_CTX):
            where_of[stretch[c * N_DP + slot]] = u * N_CTX + c
    for shift in range(N_DP):
        slot = recv[r, replica(r, -shift)]
        for d in range(PIECES):
            position = stretch[(first + d) * N_DP + slot]
            for m in range(BEHIND):
                source = where_of[jnp.maximum(position - BEHIND + m, 0)]
                out_ref[d, shift * BEHIND + m] = held[source]


def sum_windows(me, recv, stretch, held, out_ref, where_of):
    r = me[0]
    first = (me[1] // PIECES) * PIECES
    for position in range(NB):
        where_of[position] = -1
    for shift in range(N_DP):
        slot = recv[r, replica(r, -shift)]
        for d in range(PIECES):
            where_of[stretch[(first + d) * N_DP + slot]] = d * ENTRIES + shift * BEHIND
    for s in range(NB):
        position = stretch[s]
        total = jnp.zeros((BLOCK_POSITIONS, HEAD_SIZE), jnp.float32)
        for ahead in range(1, BEHIND + 1):
            reader = position + ahead
            entry = where_of[jnp.minimum(reader, NB - 1)]
            here = (reader < NB) & (entry >= 0)
            term = held[jnp.maximum(entry, 0) + (BEHIND - ahead)].astype(jnp.float32)
            total = total + jnp.where(here, term, 0.0)
        out_ref[s] = total.astype(jnp.bfloat16)


def finish(held, own, k_out, v_out):
    for piece in range(PIECES):
        target = k_out if piece < KEY_VALUE_HEADS else v_out
        column = (piece % KEY_VALUE_HEADS) * HEAD_SIZE
        for j in range(N_DP):
            at = slice(j * BLOCK_POSITIONS, (j + 1) * BLOCK_POSITIONS)
            total = own[at, piece * HEAD_SIZE : (piece + 1) * HEAD_SIZE]
            for c in range(piece, N_CTX, PIECES):
                total = total + held[c * N_DP + j].astype(jnp.float32)
            target[at, column : column + HEAD_SIZE] = total.astype(jnp.bfloat16)


def dot(a, b, dims):
    return lax.dot_general(a, b, ((dims[:1], dims[1:]), ((), ())), preferred_element_type=jnp.float32)


def window_of(win, x, shift, head, own_at):
    parts = [win[head, shift * BEHIND + m] for m in range(BEHIND)]
    return jnp.concatenate(parts + [x[:, own_at : own_at + HEAD_SIZE]], axis=0)


def stacked(x, base, head):
    at = base + head * GROUP * HEAD_SIZE
    parts = [x[:, at + i * HEAD_SIZE : at + (i + 1) * HEAD_SIZE] for i in range(GROUP)]
    return jnp.concatenate(parts, axis=0)


def unstack(target, slot, head, tall):
    for i in range(GROUP):
        at = (head * GROUP + i) * HEAD_SIZE
        target[rows(slot), at : at + HEAD_SIZE] = tall[i * BLOCK_POSITIONS : (i + 1) * BLOCK_POSITIONS]


def forward(me, recv, stretch, x0, x1, x2, x3, docs, win, attn_a, attn_b, probs_out):
    r = me[0]
    key_at = lax.broadcasted_iota(jnp.int32, (SPAN, SPAN), 0)
    query_at = lax.broadcasted_iota(jnp.int32, (SPAN, SPAN), 1) % BLOCK_POSITIONS
    causal = key_at <= query_at + BEHIND * BLOCK_POSITIONS
    for shift, x in enumerate((x0, x1, x2, x3)):
        slot = recv[r, replica(r, -shift)]
        row = docs[pl.ds(stretch[me[1] * N_DP + slot], 1), :]
        key_doc = jnp.transpose(jnp.broadcast_to(row, (SPAN, SPAN)))
        query_doc = jnp.tile(row[:, BEHIND * BLOCK_POSITIONS :], (1, SPAN // BLOCK_POSITIONS))
        bias = jnp.where((key_doc == query_doc) & causal, 0.0, -1e30)
        bias = jnp.concatenate([bias, bias], axis=1)
        for head in range(KEY_VALUE_HEADS):
            key = window_of(win, x, shift, head, K_AT + head * HEAD_SIZE)
            value = window_of(win, x, shift, head + KEY_VALUE_HEADS, V_AT + head * HEAD_SIZE)
            logits = dot(key, stacked(x, 0, head), (1, 1)) * (SCALE * LOG2_E) + bias
            weights = jnp.exp2(logits - jnp.max(logits, axis=0, keepdims=True))
            probs = weights * (1.0 / jnp.sum(weights, axis=0, keepdims=True))
            probs_out[shift * KEY_VALUE_HEADS + head] = probs
            out = dot(probs.astype(jnp.bfloat16), value, (0, 0)).astype(jnp.bfloat16)
            unstack(attn_a if head < SPLIT else attn_b, slot, head if head < SPLIT else head - SPLIT, out)


def backward(me, recv, x0, x1, x2, x3, y0, y1, y2, y3, win, probs_in, dq, sends, own):
    r = me[0]
    for shift, (x, y) in enumerate(((x0, y0), (x1, y1), (x2, y2), (x3, y3))):
        slot = recv[r, replica(r, -shift)]
        for head in range(KEY_VALUE_HEADS):
            key = window_of(win, x, shift, head, K_AT + head * HEAD_SIZE)
            value = window_of(win, x, shift, head + KEY_VALUE_HEADS, V_AT + head * HEAD_SIZE)
            query = stacked(x, 0, head)
            grad = stacked(y, 0, head)
            probs = probs_in[shift * KEY_VALUE_HEADS + head]
            low = probs.astype(jnp.bfloat16)
            dprob = dot(value, grad, (1, 1))
            delta = jnp.sum(low.astype(jnp.float32) * dprob, axis=0, keepdims=True)
            dlogit = (probs * (dprob - delta)).astype(jnp.bfloat16)
            unstack(dq, slot, head, (dot(dlogit, key, (0, 0)) * SCALE).astype(jnp.bfloat16))
            for column, term in (
                (head, dot(dlogit, query, (1, 0)) * SCALE),
                (head + KEY_VALUE_HEADS, dot(low, grad, (1, 0))),
            ):
                term_low = term[: BEHIND * BLOCK_POSITIONS].astype(jnp.bfloat16)
                for m in range(BEHIND):
                    sends[column, shift * BEHIND + m] = term_low[m * BLOCK_POSITIONS : (m + 1) * BLOCK_POSITIONS]
                own[rows(slot), column * HEAD_SIZE : (column + 1) * HEAD_SIZE] = term[BEHIND * BLOCK_POSITIONS :]


def hold(kept, kept_too, arrived, *outs):
    pass


def stage(slots, body, shapes, *operands):
    def never(*operands):
        blank = [jnp.zeros(x.shape, x.dtype) for x in shapes]
        return blank[0] if len(blank) == 1 else blank

    def always(*operands):
        result = body(*operands)
        return list(result) if isinstance(result, (list, tuple)) else result

    return lax.cond(slots[0, 0] >= 0, always, never, *operands)


def window_docs(docs):
    padded = jnp.concatenate([jnp.full((BEHIND * BLOCK_POSITIONS,), -1, jnp.int32), docs])
    padded = padded.reshape(NB + BEHIND, BLOCK_POSITIONS)
    return jnp.concatenate([padded[m : m + NB] for m in range(BEHIND + 1)], axis=1)


def on_device(queries, keys, values, out_grad, send_slot, recv_slot, stretch_block, doc_ids):
    me = jnp.stack([lax.axis_index("dp"), lax.axis_index("ctx")]).astype(jnp.int32)
    q, k, v, g = queries[0, 0], keys[0, 0], values[0, 0], out_grad[0, 0]
    stretch = stretch_block[0, 0]
    tokens = q.shape[0]
    n_section = lax.axis_size("section")

    pieces, *payloads = call(
        pack,
        [bf16(N_DP * N_CTX, BLOCK_POSITIONS, HEAD_SIZE)]
        + [bf16(BLOCK_POSITIONS, PAYLOAD)] * N_DP
        + [bf16(BLOCK_POSITIONS, QW)] * N_DP,
        [SMEM, SMEM] + [ANY] * 4,
        [pltpu.VMEM((tokens, KW), jnp.bfloat16)] * 2 + [pltpu.SemaphoreType.DMA((2 + 2 * N_DP,))],
        nbytes=9 << 19,
    )(me, send_slot, *(pltpu.with_memory_space_constraint(x, pltpu.HBM) for x in (q, g, k, v)))
    held = lax.all_to_all(pieces, ("dp", "ctx"), 0, 0, tiled=True)
    for at in range(2 * N_DP):
        if at % N_DP:
            route = [(i, (i + at) % N_DP) for i in range(N_DP)]
            payloads[at] = lax.ppermute(payloads[at], "dp", route)
    blocks, grads = payloads[:N_DP], payloads[N_DP:]
    table = [pltpu.SMEM((NB,), jnp.int32)]
    halves = [list(range(at, at + PIECES)) for at in range(0, N_CTX, PIECES)]
    entries = bf16(PIECES, ENTRIES, BLOCK_POSITIONS, HEAD_SIZE)
    group = bf16(NB, BLOCK_POSITIONS, HEAD_SIZE)
    wanted = call(gather_windows, entries, [SMEM] * 3 + [VMEM] + [ANY] * 2, table)(
        me, recv_slot, stretch, held, blocks[1], blocks[3]
    )
    windows = lax.all_to_all(wanted, "ctx", 0, 0, tiled=True, axis_index_groups=halves)
    docs = window_docs(doc_ids[0, 0])
    attn_a, attn_b, probs = call(
        forward,
        [bf16(tokens, SPLIT * HEAD_SIZE * GROUP), bf16(tokens, QW - SPLIT * HEAD_SIZE * GROUP)]
        + [jax.ShapeDtypeStruct((N_DP * KEY_VALUE_HEADS, SPAN, GROUP * BLOCK_POSITIONS), jnp.float32)],
        [SMEM] * 3 + [VMEM] * 6,
        flops=1 << 29,
        nbytes=6 << 20,
    )(me, recv_slot, stretch, *blocks, docs, windows)
    onward = [(i, (i + 1) % n_section) for i in range(n_section)]
    handoff_a = lax.ppermute(attn_a, "section", onward)

    def sum_gradients(blocks, windows, probs):
        q_grad, sends, own = call(
            backward,
            [bf16(tokens, QW), entries, jax.ShapeDtypeStruct((tokens, 2 * KW), jnp.float32)],
            [SMEM] * 2 + [VMEM] * 10,
            flops=1 << 30,
            nbytes=6 << 20,
        )(me, recv_slot, *blocks, windows, probs)
        partial = lax.all_to_all(sends, "ctx", 0, 0, tiled=True, axis_index_groups=halves)
        summed = call(sum_windows, group, [SMEM] * 3 + [VMEM], table)(
            me, recv_slot, stretch, partial.reshape(PIECES * ENTRIES, BLOCK_POSITIONS, HEAD_SIZE)
        )
        return q_grad, summed, own

    q_grad, summed, own = stage(
        send_slot,
        sum_gradients,
        [bf16(tokens, QW), group, jax.ShapeDtypeStruct((tokens, 2 * KW), jnp.float32)],
        payloads,
        windows,
        probs,
    )
    summed, attn_b = call(
        hold, [group, bf16(*attn_b.shape)], [ANY] * 3, out_space=ANY, aliases={0: 0, 1: 1}
    )(summed, attn_b, handoff_a)
    handoff_b = lax.ppermute(attn_b, "section", onward)

    def own_gradients(summed, own):
        back = lax.all_to_all(summed.reshape(N_CTX, N_DP, BLOCK_POSITIONS, HEAD_SIZE), "ctx", 0, 0, tiled=True)
        return call(finish, [bf16(tokens, KW)] * 2, [VMEM] * 2)(
            back.reshape(NB, BLOCK_POSITIONS, HEAD_SIZE), own
        )

    k_grad, v_grad = stage(send_slot, own_gradients, [bf16(tokens, KW)] * 2, summed, own)
    handoff = jnp.concatenate([handoff_a, handoff_b], axis=1)
    return handoff[None, None], q_grad[None, None], k_grad[None, None], v_grad[None, None]


def solution(mesh):
    tokens = P("dp", "section", "ctx", None)
    row = P("dp", "section", None)
    return jax.shard_map(
        on_device,
        mesh=mesh,
        in_specs=(tokens, tokens, tokens, tokens, P(), P(), row, row),
        out_specs=(tokens, tokens, tokens, tokens),
        check_vma=False,
    )
```

```python
import math

import jax
import jax.numpy as jnp
from jax import lax
from jax.experimental import pallas as pl
from jax.experimental.pallas import tpu as pltpu
from jax.sharding import PartitionSpec as P

QUERY_HEADS = 32
KEY_VALUE_HEADS = 4
HEAD_SIZE = 128
BLOCK_POSITIONS = 32
N_DP = 4
N_CTX = 16
NB = 64
GROUP = QUERY_HEADS // KEY_VALUE_HEADS
QW = QUERY_HEADS * HEAD_SIZE
KW = KEY_VALUE_HEADS * HEAD_SIZE
K_AT = QW
V_AT = QW + KW
PAYLOAD = QW + 2 * KW
PIECES = 2 * KEY_VALUE_HEADS
PARTS = ((0, 1), (2,), (3,))
BEHIND = 3
ENTRIES = N_DP * BEHIND
SCALE = HEAD_SIZE ** (-0.5)
LOG2_E = math.log2(math.e)
SPAN = (BEHIND + 1) * BLOCK_POSITIONS

VMEM = pl.BlockSpec(memory_space=pltpu.VMEM)
SMEM = pl.BlockSpec(memory_space=pltpu.SMEM)
ANY = pl.BlockSpec(memory_space=pl.ANY)
HBM = pl.BlockSpec(memory_space=pltpu.HBM)


def call(
    kernel, out_shape, in_specs, scratch=(), flops=0, nbytes=1 << 20, out_space=VMEM, aliases={}, limit=40
):
    if isinstance(out_shape, list) and not isinstance(out_space, list):
        out_space = [out_space] * len(out_shape)
    return pl.pallas_call(
        kernel,
        out_shape=out_shape,
        in_specs=in_specs,
        out_specs=out_space,
        scratch_shapes=scratch,
        input_output_aliases=aliases,
        compiler_params=pltpu.CompilerParams(vmem_limit_bytes=limit << 20),
        cost_estimate=pl.CostEstimate(flops=flops, bytes_accessed=nbytes, transcendentals=0),
    )


def bf16(*shape):
    return jax.ShapeDtypeStruct(shape, jnp.bfloat16)


def replica(me, shift):
    return lax.rem(me + shift + N_DP, N_DP)


def rows(block):
    return pl.ds(pl.multiple_of(block * BLOCK_POSITIONS, BLOCK_POSITIONS), BLOCK_POSITIONS)


def pack(me, send, q_ref, g_ref, k_ref, v_ref, pieces, *refs):
    mains, (grads, k_rows, v_rows, sems) = refs[:N_DP], refs[N_DP:]
    r = me[0]
    copies = [
        pltpu.make_async_copy(k_ref, k_rows, sems.at[0]),
        pltpu.make_async_copy(v_ref, v_rows, sems.at[1]),
    ]
    for shift in (1, 3, 2, 0):
        source = rows(send[r, replica(r, shift)])
        for ref, target in ((q_ref, mains[shift].at[:, :QW]), (g_ref, grads.at[replica(r, shift)])):
            copies.append(pltpu.make_async_copy(ref.at[source], target, sems.at[len(copies)]))
    for copy in copies:
        copy.start()
    copies[0].wait()
    copies[1].wait()
    for u in range(N_DP):
        block = send[r, u]
        for piece in range(PIECES):
            source = k_rows if piece < KEY_VALUE_HEADS else v_rows
            column = (piece % KEY_VALUE_HEADS) * HEAD_SIZE
            part = source[rows(block), column : column + HEAD_SIZE]
            for c in range(piece, N_CTX, PIECES):
                pieces[u * N_CTX + c] = part
    for shift, target in enumerate(mains):
        block = send[r, replica(r, shift)]
        target[:, K_AT:V_AT] = k_rows[rows(block), :]
        target[:, V_AT:] = v_rows[rows(block), :]
    for copy in copies[2:]:
        copy.wait()


def gather_windows(me, recv, stretch, held, after, before, out_ref, where_of):
    r = me[0]
    first = (me[1] // PIECES) * PIECES
    for u in range(N_DP):
        slot = recv[r, u]
        for c in range(N_CTX):
            where_of[stretch[c * N_DP + slot]] = u * N_CTX + c
    for shift in range(N_DP):
        slot = recv[r, replica(r, -shift)]
        for d in range(PIECES):
            position = stretch[(first + d) * N_DP + slot]
            for m in range(BEHIND):
                source = where_of[jnp.maximum(position - BEHIND + m, 0)]
                out_ref[d, shift * BEHIND + m] = held[source]


def sum_windows(me, recv, stretch, held, out_ref, where_of):
    r = me[0]
    first = (me[1] // PIECES) * PIECES
    for position in range(NB):
        where_of[position] = -1
    for shift in range(N_DP):
        slot = recv[r, replica(r, -shift)]
        for d in range(PIECES):
            where_of[stretch[(first + d) * N_DP + slot]] = d * ENTRIES + shift * BEHIND
    for s in range(NB):
        position = stretch[s]
        total = jnp.zeros((BLOCK_POSITIONS, HEAD_SIZE), jnp.float32)
        for ahead in range(1, BEHIND + 1):
            reader = position + ahead
            entry = where_of[jnp.minimum(reader, NB - 1)]
            here = (reader < NB) & (entry >= 0)
            term = held[jnp.maximum(entry, 0) + (BEHIND - ahead)].astype(jnp.float32)
            total = total + jnp.where(here, term, 0.0)
        out_ref[s] = total.astype(jnp.bfloat16)


def finish(held, own, k_out, v_out):
    for piece in range(PIECES):
        target = k_out if piece < KEY_VALUE_HEADS else v_out
        column = (piece % KEY_VALUE_HEADS) * HEAD_SIZE
        for j in range(N_DP):
            at = slice(j * BLOCK_POSITIONS, (j + 1) * BLOCK_POSITIONS)
            total = own[at, piece * HEAD_SIZE : (piece + 1) * HEAD_SIZE]
            for c in range(piece, N_CTX, PIECES):
                total = total + held[c * N_DP + j].astype(jnp.float32)
            target[at, column : column + HEAD_SIZE] = total.astype(jnp.bfloat16)


def dot(a, b, dims):
    return lax.dot_general(a, b, ((dims[:1], dims[1:]), ((), ())), preferred_element_type=jnp.float32)


def window_of(win, x, shift, head, own_at):
    parts = [win[head, shift * BEHIND + m] for m in range(BEHIND)]
    return jnp.concatenate(parts + [x[:, own_at : own_at + HEAD_SIZE]], axis=0)


def stacked(x, base, head):
    at = base + head * GROUP * HEAD_SIZE
    parts = [x[:, at + i * HEAD_SIZE : at + (i + 1) * HEAD_SIZE] for i in range(GROUP)]
    return jnp.concatenate(parts, axis=0)


def unstack(target, slot, head, tall):
    for i in range(GROUP):
        at = (head * GROUP + i) * HEAD_SIZE
        target[rows(slot), at : at + HEAD_SIZE] = tall[i * BLOCK_POSITIONS : (i + 1) * BLOCK_POSITIONS]


def forward(me, recv, stretch, x0, x1, x2, x3, docs, win, *outs):
    r = me[0]
    key_at = lax.broadcasted_iota(jnp.int32, (SPAN, SPAN), 0)
    query_at = lax.broadcasted_iota(jnp.int32, (SPAN, SPAN), 1) % BLOCK_POSITIONS
    causal = key_at <= query_at + BEHIND * BLOCK_POSITIONS
    for shift, x in enumerate((x0, x1, x2, x3)):
        slot = recv[r, replica(r, -shift)]
        row = docs[pl.ds(stretch[me[1] * N_DP + slot], 1), :]
        key_doc = jnp.transpose(jnp.broadcast_to(row, (SPAN, SPAN)))
        query_doc = jnp.tile(row[:, BEHIND * BLOCK_POSITIONS :], (1, SPAN // BLOCK_POSITIONS))
        bias = jnp.where((key_doc == query_doc) & causal, 0.0, -1e30)
        bias = jnp.concatenate([bias, bias], axis=1)
        for head in range(KEY_VALUE_HEADS):
            key = window_of(win, x, shift, head, K_AT + head * HEAD_SIZE)
            value = window_of(win, x, shift, head + KEY_VALUE_HEADS, V_AT + head * HEAD_SIZE)
            logits = dot(key, stacked(x, 0, head), (1, 1)) * (SCALE * LOG2_E) + bias
            weights = jnp.exp2(logits - jnp.max(logits, axis=0, keepdims=True))
            probs = weights * (1.0 / jnp.sum(weights, axis=0, keepdims=True))
            low = probs.astype(jnp.bfloat16)
            outs[-1][shift * KEY_VALUE_HEADS + head] = low
            out = dot(low, value, (0, 0)).astype(jnp.bfloat16)
            part = [head in heads for heads in PARTS].index(True)
            unstack(outs[part], slot, PARTS[part].index(head), out)


def backward(me, recv, x0, x1, x2, x3, grads, win, probs_in, dq, sends, own):
    r = me[0]
    for shift, x in enumerate((x0, x1, x2, x3)):
        slot = recv[r, replica(r, -shift)]
        for head in range(KEY_VALUE_HEADS):
            key = window_of(win, x, shift, head, K_AT + head * HEAD_SIZE)
            value = window_of(win, x, shift, head + KEY_VALUE_HEADS, V_AT + head * HEAD_SIZE)
            query = stacked(x, 0, head)
            grad = stacked(grads.at[replica(r, -shift)], 0, head)
            low = probs_in[shift * KEY_VALUE_HEADS + head]
            probs = low.astype(jnp.float32)
            dprob = dot(value, grad, (1, 1))
            delta = jnp.sum(probs * dprob, axis=0, keepdims=True)
            dlogit = (probs * (dprob - delta)).astype(jnp.bfloat16)
            unstack(dq, slot, head, (dot(dlogit, key, (0, 0)) * SCALE).astype(jnp.bfloat16))
            for column, term in (
                (head, dot(dlogit, query, (1, 0)) * SCALE),
                (head + KEY_VALUE_HEADS, dot(low, grad, (1, 0))),
            ):
                term_low = term[: BEHIND * BLOCK_POSITIONS].astype(jnp.bfloat16)
                for m in range(BEHIND):
                    sends[column, shift * BEHIND + m] = term_low[m * BLOCK_POSITIONS : (m + 1) * BLOCK_POSITIONS]
                own[rows(slot), column * HEAD_SIZE : (column + 1) * HEAD_SIZE] = term[BEHIND * BLOCK_POSITIONS :]


def hold(kept, kept_too, arrived, arrived_too, *outs):
    pass


def stage(me, body, shapes, *operands):
    def never(*operands):
        blank = [jnp.zeros(x.shape, x.dtype) for x in shapes]
        return blank[0] if len(blank) == 1 else blank

    def always(*operands):
        result = body(*operands)
        return list(result) if isinstance(result, (list, tuple)) else result

    return lax.cond(me[0] >= 0, always, never, *operands)


def window_docs(docs):
    padded = jnp.concatenate([jnp.full((BEHIND * BLOCK_POSITIONS,), -1, jnp.int32), docs])
    padded = padded.reshape(NB + BEHIND, BLOCK_POSITIONS)
    return jnp.concatenate([padded[m : m + NB] for m in range(BEHIND + 1)], axis=1)


def on_device(queries, keys, values, out_grad, send_slot, recv_slot, stretch_block, doc_ids):
    me = jnp.stack([lax.axis_index("dp"), lax.axis_index("ctx")]).astype(jnp.int32)
    q, k, v, g = queries[0, 0], keys[0, 0], values[0, 0], out_grad[0, 0]
    stretch = stretch_block[0, 0]
    tokens = q.shape[0]
    n_section = lax.axis_size("section")

    pieces, *payloads = call(
        pack,
        [bf16(N_DP * N_CTX, BLOCK_POSITIONS, HEAD_SIZE)]
        + [bf16(BLOCK_POSITIONS, PAYLOAD)] * N_DP
        + [bf16(N_DP, BLOCK_POSITIONS, QW)],
        [SMEM, SMEM] + [ANY] * 4,
        [pltpu.VMEM((tokens, KW), jnp.bfloat16)] * 2 + [pltpu.SemaphoreType.DMA((2 + 2 * N_DP,))],
        nbytes=9 << 19,
    )(me, send_slot, *(pltpu.with_memory_space_constraint(x, pltpu.HBM) for x in (q, g, k, v)))
    held = lax.all_to_all(pieces, ("dp", "ctx"), 0, 0, tiled=True)
    grads = payloads[N_DP]
    blocks = [payloads[0]] + [
        lax.ppermute(payloads[at], "dp", [(i, (i + at) % N_DP) for i in range(N_DP)]) for at in range(1, N_DP)
    ]
    table = [pltpu.SMEM((NB,), jnp.int32)]
    halves = [list(range(at, at + PIECES)) for at in range(0, N_CTX, PIECES)]
    entries = bf16(PIECES, ENTRIES, BLOCK_POSITIONS, HEAD_SIZE)
    group = bf16(NB, BLOCK_POSITIONS, HEAD_SIZE)
    wanted = call(gather_windows, entries, [SMEM] * 3 + [VMEM] + [ANY] * 2, table)(
        me, recv_slot, stretch, held, blocks[1], blocks[3]
    )
    windows = lax.all_to_all(wanted, "ctx", 0, 0, tiled=True, axis_index_groups=halves)
    grads = lax.all_to_all(grads, "dp", 0, 0, tiled=True)
    docs = window_docs(doc_ids[0, 0])
    attn_a, attn_b, attn_c, probs = call(
        forward,
        [bf16(tokens, len(heads) * HEAD_SIZE * GROUP) for heads in PARTS]
        + [bf16(N_DP * KEY_VALUE_HEADS, SPAN, GROUP * BLOCK_POSITIONS)],
        [SMEM] * 3 + [VMEM] * 6,
        flops=1 << 29,
        nbytes=6 << 20,
    )(me, recv_slot, stretch, *blocks, docs, windows)
    onward = [(i, (i + 1) % n_section) for i in range(n_section)]
    odd = range(1, n_section, 2)
    around = [(i, (i - 2) % n_section) for i in odd]
    last = [(i, (i - 3) % n_section) for i in odd] + [(i - 1, i) for i in odd]
    handoff_a = lax.ppermute(attn_a, "section", onward)
    relay = lax.ppermute(attn_c, "section", around)
    relay = lax.ppermute(relay, "section", around)

    def sum_gradients(blocks, windows, probs):
        q_grad, sends, own = call(
            backward,
            [bf16(tokens, QW), entries, jax.ShapeDtypeStruct((tokens, 2 * KW), jnp.float32)],
            [SMEM] * 2 + [VMEM] * 7,
            flops=1 << 30,
            nbytes=6 << 20,
        )(me, recv_slot, *blocks, windows, probs)
        partial = lax.all_to_all(sends, "ctx", 0, 0, tiled=True, axis_index_groups=halves)
        summed = call(sum_windows, group, [SMEM] * 3 + [VMEM], table)(
            me, recv_slot, stretch, partial.reshape(PIECES * ENTRIES, BLOCK_POSITIONS, HEAD_SIZE)
        )
        return q_grad, summed, own

    q_grad, summed, own = stage(
        me,
        sum_gradients,
        [bf16(tokens, QW), group, jax.ShapeDtypeStruct((tokens, 2 * KW), jnp.float32)],
        [*blocks, grads],
        windows,
        probs,
    )
    summed, attn_b = call(
        hold, [group, bf16(*attn_b.shape)], [ANY] * 4, out_space=ANY, aliases={0: 0, 1: 1}
    )(summed, attn_b, handoff_a, relay)
    handoff_b = lax.ppermute(attn_b, "section", onward)
    relay = jnp.where(lax.axis_index("section") % 2 == 1, relay, attn_c)
    handoff_c = lax.ppermute(relay, "section", last)

    def own_gradients(summed, own):
        back = lax.all_to_all(summed.reshape(N_CTX, N_DP, BLOCK_POSITIONS, HEAD_SIZE), "ctx", 0, 0, tiled=True)
        return call(finish, [bf16(tokens, KW)] * 2, [VMEM] * 2)(
            back.reshape(NB, BLOCK_POSITIONS, HEAD_SIZE), own
        )

    k_grad, v_grad = stage(me, own_gradients, [bf16(tokens, KW)] * 2, summed, own)
    handoff = jnp.concatenate([handoff_a, handoff_b, handoff_c], axis=1)
    return handoff[None, None], q_grad[None, None], k_grad[None, None], v_grad[None, None]


def solution(mesh):
    tokens = P("dp", "section", "ctx", None)
    row = P("dp", "section", None)
    return jax.shard_map(
        on_device,
        mesh=mesh,
        in_specs=(tokens, tokens, tokens, tokens, P(), P(), row, row),
        out_specs=(tokens, tokens, tokens, tokens),
        check_vma=False,
    )
```

```python
import math

import jax
import jax.numpy as jnp
from jax import lax
from jax.experimental import pallas as pl
from jax.experimental.pallas import tpu as pltpu
from jax.sharding import PartitionSpec as P

QUERY_HEADS = 32
KEY_VALUE_HEADS = 4
HEAD_SIZE = 128
BLOCK_POSITIONS = 32
N_DP = 4
N_CTX = 16
NB = 64
GROUP = QUERY_HEADS // KEY_VALUE_HEADS
QW = QUERY_HEADS * HEAD_SIZE
KW = KEY_VALUE_HEADS * HEAD_SIZE
K_AT = QW
V_AT = QW + KW
PAYLOAD = QW + 2 * KW
PIECES = 2 * KEY_VALUE_HEADS
PARTS = ((0, 1), (2,), (3,))
BEHIND = 3
ENTRIES = N_DP * BEHIND
SCALE = HEAD_SIZE ** (-0.5)
LOG2_E = math.log2(math.e)
SPAN = (BEHIND + 1) * BLOCK_POSITIONS

VMEM = pl.BlockSpec(memory_space=pltpu.VMEM)
SMEM = pl.BlockSpec(memory_space=pltpu.SMEM)
ANY = pl.BlockSpec(memory_space=pl.ANY)
HBM = pl.BlockSpec(memory_space=pltpu.HBM)


def call(
    kernel, out_shape, in_specs, scratch=(), flops=0, nbytes=1 << 20, out_space=VMEM, aliases={}, limit=20
):
    if isinstance(out_shape, list) and not isinstance(out_space, list):
        out_space = [out_space] * len(out_shape)
    return pl.pallas_call(
        kernel,
        out_shape=out_shape,
        in_specs=in_specs,
        out_specs=out_space,
        scratch_shapes=scratch,
        input_output_aliases=aliases,
        compiler_params=pltpu.CompilerParams(vmem_limit_bytes=limit << 20),
        cost_estimate=pl.CostEstimate(flops=flops, bytes_accessed=nbytes, transcendentals=0),
    )


def bf16(*shape):
    return jax.ShapeDtypeStruct(shape, jnp.bfloat16)


def replica(me, shift):
    return lax.rem(me + shift + N_DP, N_DP)


def rows(block):
    return pl.ds(pl.multiple_of(block * BLOCK_POSITIONS, BLOCK_POSITIONS), BLOCK_POSITIONS)


def pack(me, send, q_ref, g_ref, k_ref, v_ref, pieces, *refs):
    mains, (grads, k_rows, v_rows, sems) = refs[:N_DP], refs[N_DP:]
    r = me[0]
    copies = [
        pltpu.make_async_copy(k_ref, k_rows, sems.at[0]),
        pltpu.make_async_copy(v_ref, v_rows, sems.at[1]),
    ]
    for shift in (1, 3, 2, 0):
        source = rows(send[r, replica(r, shift)])
        for ref, target in ((q_ref, mains[shift].at[:, :QW]), (g_ref, grads.at[replica(r, shift)])):
            copies.append(pltpu.make_async_copy(ref.at[source], target, sems.at[len(copies)]))
    for copy in copies:
        copy.start()
    copies[0].wait()
    copies[1].wait()
    for u in range(N_DP):
        block = send[r, u]
        for piece in range(PIECES):
            source = k_rows if piece < KEY_VALUE_HEADS else v_rows
            column = (piece % KEY_VALUE_HEADS) * HEAD_SIZE
            part = source[rows(block), column : column + HEAD_SIZE]
            for c in range(piece, N_CTX, PIECES):
                pieces[u * N_CTX + c] = part
    for shift, target in enumerate(mains):
        block = send[r, replica(r, shift)]
        target[:, K_AT:V_AT] = k_rows[rows(block), :]
        target[:, V_AT:] = v_rows[rows(block), :]
    for copy in copies[2:]:
        copy.wait()


def gather_windows(me, recv, stretch, held, after, before, out_ref, where_of):
    r = me[0]
    first = (me[1] // PIECES) * PIECES
    for u in range(N_DP):
        slot = recv[r, u]
        for c in range(N_CTX):
            where_of[stretch[c * N_DP + slot]] = u * N_CTX + c
    for shift in range(N_DP):
        slot = recv[r, replica(r, -shift)]
        for d in range(PIECES):
            position = stretch[(first + d) * N_DP + slot]
            for m in range(BEHIND):
                source = where_of[jnp.maximum(position - BEHIND + m, 0)]
                out_ref[d, shift * BEHIND + m] = held[source]


def sum_windows(me, recv, stretch, held, out_ref, where_of):
    r = me[0]
    first = (me[1] // PIECES) * PIECES
    for position in range(NB):
        where_of[position] = -1
    for shift in range(N_DP):
        slot = recv[r, replica(r, -shift)]
        for d in range(PIECES):
            where_of[stretch[(first + d) * N_DP + slot]] = d * ENTRIES + shift * BEHIND
    for s in range(NB):
        position = stretch[s]
        total = jnp.zeros((BLOCK_POSITIONS, HEAD_SIZE), jnp.float32)
        for ahead in range(1, BEHIND + 1):
            reader = position + ahead
            entry = where_of[jnp.minimum(reader, NB - 1)]
            here = (reader < NB) & (entry >= 0)
            term = held[jnp.maximum(entry, 0) + (BEHIND - ahead)].astype(jnp.float32)
            total = total + jnp.where(here, term, 0.0)
        out_ref[s] = total.astype(jnp.bfloat16)


def finish(held, own, k_out, v_out):
    for piece in range(PIECES):
        target = k_out if piece < KEY_VALUE_HEADS else v_out
        column = (piece % KEY_VALUE_HEADS) * HEAD_SIZE
        for j in range(N_DP):
            at = slice(j * BLOCK_POSITIONS, (j + 1) * BLOCK_POSITIONS)
            total = own[at, piece * HEAD_SIZE : (piece + 1) * HEAD_SIZE]
            for c in range(piece, N_CTX, PIECES):
                total = total + held[c * N_DP + j].astype(jnp.float32)
            target[at, column : column + HEAD_SIZE] = total.astype(jnp.bfloat16)


def dot(a, b, dims):
    return lax.dot_general(a, b, ((dims[:1], dims[1:]), ((), ())), preferred_element_type=jnp.float32)


def window_of(win, x, shift, head, own_at):
    parts = [win[head, shift * BEHIND + m] for m in range(BEHIND)]
    return jnp.concatenate(parts + [x[:, own_at : own_at + HEAD_SIZE]], axis=0)


def stacked(x, base, head):
    at = base + head * GROUP * HEAD_SIZE
    parts = [x[:, at + i * HEAD_SIZE : at + (i + 1) * HEAD_SIZE] for i in range(GROUP)]
    return jnp.concatenate(parts, axis=0)


def unstack(target, slot, head, tall):
    for i in range(GROUP):
        at = (head * GROUP + i) * HEAD_SIZE
        target[rows(slot), at : at + HEAD_SIZE] = tall[i * BLOCK_POSITIONS : (i + 1) * BLOCK_POSITIONS]


def forward(me, recv, stretch, x0, x1, x2, x3, docs, win, *outs):
    r = me[0]
    key_at = lax.broadcasted_iota(jnp.int32, (SPAN, SPAN), 0)
    query_at = lax.broadcasted_iota(jnp.int32, (SPAN, SPAN), 1) % BLOCK_POSITIONS
    causal = key_at <= query_at + BEHIND * BLOCK_POSITIONS
    for shift, x in enumerate((x0, x1, x2, x3)):
        slot = recv[r, replica(r, -shift)]
        row = docs[pl.ds(stretch[me[1] * N_DP + slot], 1), :]
        key_doc = jnp.transpose(jnp.broadcast_to(row, (SPAN, SPAN)))
        query_doc = jnp.tile(row[:, BEHIND * BLOCK_POSITIONS :], (1, SPAN // BLOCK_POSITIONS))
        bias = jnp.where((key_doc == query_doc) & causal, 0.0, -1e30)
        bias = jnp.concatenate([bias, bias], axis=1)
        for head in range(KEY_VALUE_HEADS):
            key = window_of(win, x, shift, head, K_AT + head * HEAD_SIZE)
            value = window_of(win, x, shift, head + KEY_VALUE_HEADS, V_AT + head * HEAD_SIZE)
            logits = dot(key, stacked(x, 0, head), (1, 1)) * (SCALE * LOG2_E) + bias
            weights = jnp.exp2(logits - jnp.max(logits, axis=0, keepdims=True))
            probs = weights * (1.0 / jnp.sum(weights, axis=0, keepdims=True))
            low = probs.astype(jnp.bfloat16)
            outs[-1][shift * KEY_VALUE_HEADS + head] = low
            out = dot(low, value, (0, 0)).astype(jnp.bfloat16)
            part = [head in heads for heads in PARTS].index(True)
            unstack(outs[part], slot, PARTS[part].index(head), out)


def backward(me, recv, x0, x1, x2, x3, grads, win, probs_in, dq, sends, own):
    r = me[0]
    for shift, x in enumerate((x0, x1, x2, x3)):
        slot = recv[r, replica(r, -shift)]
        for head in range(KEY_VALUE_HEADS):
            key = window_of(win, x, shift, head, K_AT + head * HEAD_SIZE)
            value = window_of(win, x, shift, head + KEY_VALUE_HEADS, V_AT + head * HEAD_SIZE)
            query = stacked(x, 0, head)
            grad = stacked(grads.at[replica(r, -shift)], 0, head)
            low = probs_in[shift * KEY_VALUE_HEADS + head]
            probs = low.astype(jnp.float32)
            dprob = dot(value, grad, (1, 1))
            delta = jnp.sum(probs * dprob, axis=0, keepdims=True)
            dlogit = (probs * (dprob - delta)).astype(jnp.bfloat16)
            unstack(dq, slot, head, (dot(dlogit, key, (0, 0)) * SCALE).astype(jnp.bfloat16))
            for column, term in (
                (head, dot(dlogit, query, (1, 0)) * SCALE),
                (head + KEY_VALUE_HEADS, dot(low, grad, (1, 0))),
            ):
                term_low = term[: BEHIND * BLOCK_POSITIONS].astype(jnp.bfloat16)
                for m in range(BEHIND):
                    sends[column, shift * BEHIND + m] = term_low[m * BLOCK_POSITIONS : (m + 1) * BLOCK_POSITIONS]
                own[rows(slot), column * HEAD_SIZE : (column + 1) * HEAD_SIZE] = term[BEHIND * BLOCK_POSITIONS :]


def hold(kept, kept_too, arrived, arrived_too, *outs):
    pass


def stage(me, body, shapes, *operands):
    def never(*operands):
        blank = [jnp.zeros(x.shape, x.dtype) for x in shapes]
        return blank[0] if len(blank) == 1 else blank

    def always(*operands):
        result = body(*operands)
        return list(result) if isinstance(result, (list, tuple)) else result

    return lax.cond(me[0] >= 0, always, never, *operands)


def window_docs(docs):
    padded = jnp.concatenate([jnp.full((BEHIND * BLOCK_POSITIONS,), -1, jnp.int32), docs])
    padded = padded.reshape(NB + BEHIND, BLOCK_POSITIONS)
    return jnp.concatenate([padded[m : m + NB] for m in range(BEHIND + 1)], axis=1)


def on_device(queries, keys, values, out_grad, send_slot, recv_slot, stretch_block, doc_ids):
    me = jnp.stack([lax.axis_index("dp"), lax.axis_index("ctx")]).astype(jnp.int32)
    q, k, v, g = queries[0, 0], keys[0, 0], values[0, 0], out_grad[0, 0]
    stretch = stretch_block[0, 0]
    tokens = q.shape[0]
    n_section = lax.axis_size("section")

    pieces, *payloads = call(
        pack,
        [bf16(N_DP * N_CTX, BLOCK_POSITIONS, HEAD_SIZE)]
        + [bf16(BLOCK_POSITIONS, PAYLOAD)] * N_DP
        + [bf16(N_DP, BLOCK_POSITIONS, QW)],
        [SMEM, SMEM] + [ANY] * 4,
        [pltpu.VMEM((tokens, KW), jnp.bfloat16)] * 2 + [pltpu.SemaphoreType.DMA((2 + 2 * N_DP,))],
        nbytes=9 << 19,
    )(me, send_slot, *(pltpu.with_memory_space_constraint(x, pltpu.HBM) for x in (q, g, k, v)))
    held = lax.all_to_all(pieces, ("dp", "ctx"), 0, 0, tiled=True)
    grads = payloads[N_DP]
    blocks = [payloads[0]] + [
        lax.ppermute(payloads[at], "dp", [(i, (i + at) % N_DP) for i in range(N_DP)]) for at in range(1, N_DP)
    ]
    table = [pltpu.SMEM((NB,), jnp.int32)]
    halves = [list(range(at, at + PIECES)) for at in range(0, N_CTX, PIECES)]
    entries = bf16(PIECES, ENTRIES, BLOCK_POSITIONS, HEAD_SIZE)
    group = bf16(NB, BLOCK_POSITIONS, HEAD_SIZE)
    wanted = call(gather_windows, entries, [SMEM] * 3 + [VMEM] + [ANY] * 2, table)(
        me, recv_slot, stretch, held, blocks[1], blocks[3]
    )
    windows = lax.all_to_all(wanted, "ctx", 0, 0, tiled=True, axis_index_groups=halves)
    grads = lax.all_to_all(grads, "dp", 0, 0, tiled=True)
    docs = window_docs(doc_ids[0, 0])
    attn_a, attn_b, attn_c, probs = call(
        forward,
        [bf16(tokens, len(heads) * HEAD_SIZE * GROUP) for heads in PARTS]
        + [bf16(N_DP * KEY_VALUE_HEADS, SPAN, GROUP * BLOCK_POSITIONS)],
        [SMEM] * 3 + [VMEM] * 6,
        flops=1 << 29,
        nbytes=6 << 20,
    )(me, recv_slot, stretch, *blocks, docs, windows)
    onward = [(i, (i + 1) % n_section) for i in range(n_section)]
    odd = range(1, n_section, 2)
    around = [(i, (i - 2) % n_section) for i in odd]
    last = [(i, (i - 3) % n_section) for i in odd] + [(i - 1, i) for i in odd]
    handoff_a = lax.ppermute(attn_a, "section", onward)
    relay = lax.ppermute(attn_c, "section", around)
    relay = lax.ppermute(relay, "section", around)

    def sum_gradients(blocks, windows, probs):
        q_grad, sends, own = call(
            backward,
            [bf16(tokens, QW), entries, jax.ShapeDtypeStruct((tokens, 2 * KW), jnp.float32)],
            [SMEM] * 2 + [VMEM] * 7,
            flops=1 << 30,
            nbytes=6 << 20,
        )(me, recv_slot, *blocks, windows, probs)
        partial = lax.all_to_all(sends, "ctx", 0, 0, tiled=True, axis_index_groups=halves)
        summed = call(sum_windows, group, [SMEM] * 3 + [VMEM], table)(
            me, recv_slot, stretch, partial.reshape(PIECES * ENTRIES, BLOCK_POSITIONS, HEAD_SIZE)
        )
        return q_grad, summed, own

    q_grad, summed, own = stage(
        me,
        sum_gradients,
        [bf16(tokens, QW), group, jax.ShapeDtypeStruct((tokens, 2 * KW), jnp.float32)],
        [*blocks, grads],
        windows,
        probs,
    )
    summed, attn_b = call(
        hold, [group, bf16(*attn_b.shape)], [ANY] * 4, out_space=ANY, aliases={0: 0, 1: 1}
    )(summed, attn_b, handoff_a, relay)
    handoff_b = lax.ppermute(attn_b, "section", onward)
    relay = jnp.where(lax.axis_index("section") % 2 == 1, relay, attn_c)
    handoff_c = lax.ppermute(relay, "section", last)

    def own_gradients(summed, own):
        back = lax.all_to_all(summed.reshape(N_CTX, N_DP, BLOCK_POSITIONS, HEAD_SIZE), "ctx", 0, 0, tiled=True)
        return call(finish, [bf16(tokens, KW)] * 2, [VMEM] * 2)(
            back.reshape(NB, BLOCK_POSITIONS, HEAD_SIZE), own
        )

    k_grad, v_grad = stage(me, own_gradients, [bf16(tokens, KW)] * 2, summed, own)
    handoff = jnp.concatenate([handoff_a, handoff_b, handoff_c], axis=1)
    return handoff[None, None], q_grad[None, None], k_grad[None, None], v_grad[None, None]


def solution(mesh):
    tokens = P("dp", "section", "ctx", None)
    row = P("dp", "section", None)
    return jax.shard_map(
        on_device,
        mesh=mesh,
        in_specs=(tokens, tokens, tokens, tokens, P(), P(), row, row),
        out_specs=(tokens, tokens, tokens, tokens),
        check_vma=False,
    )
```
